32 devices in a mesh: mx: 8 (over y, x, core), my: 4 (over z).
Axes of the slice: x: 2, y: 2, z: 4, core: 2. Of those that a mesh axis runs over, the one named last changes fastest.
Arguments:
- documents: bfloat16 [32768, 768], P(('mx', 'my')), may hold values from -12 to 12
- owner_tile: int32 [32768, 1], P(('mx', 'my')), may hold values from 0 to 31; in each aligned block of 1024 rows (0 to 1023, 1024 to 2047, ...) at most 64 rows name the same one
- unit_in_tile: int32 [32768], P(('mx', 'my')), may hold values from 0 to 4095
- codebook: bfloat16 [512, 256, 768], P('mx', 'my'), may hold values from -6 to 6
Outputs:
- new_codebook: bfloat16 [512, 256, 768], P('mx', 'my')
The draws below stay inside these ranges and needn't reach their ends.
Inputs may be any that keep to these rules, and one draw needn't show every extreme that they name: `owner_tile`: among the rows of one device no tile is named by more than 64 documents, and in every draw some tile is named by exactly 64 rows of some device.
All inputs are finite; a program needn't handle non-finite values.
Results may differ from the reference program's by a relative error of at most 0.001.
Values may be sent and summed in bfloat16 or wider, within the bound.
A program may use at most 256 MiB of HBM per device.

```python
import math
import jax
import jax.numpy as jnp
import numpy as np
from jax import lax

E = 768
TR = 64
TC = 64
RADIUS = 8
DOC_DEV = 1024
TILES = 32
CAP = 64
MR = 512
MC = 256
DOCS = 32768
N_MY = 4


def with_ends(values, own_key, smallest, high):
    longest = values.shape.index(max(values.shape))
    spots = []
    for shift in (0, 1):
        where = [jax.random.randint(jax.random.fold_in(own_key, axis), (), 0, length) for axis, length in enumerate(values.shape)]
        where[longest] = (where[longest] + shift) % values.shape[longest]
        spots.append(tuple(where))
    return values.at[spots[0]].set(smallest).at[spots[1]].set(high)


def block_scale(rng, dims, shards, least, top_value):
    factor_of = 1.0
    for dim, shards_of in shards:
        steps = jax.random.uniform(jax.random.fold_in(jax.random.fold_in(rng, 6), dim), (shards_of,), jnp.float32, least / len(shards), top_value / len(shards))
        factor_of = factor_of * jnp.repeat(jnp.exp(steps), dims[dim] // shards_of).reshape((-1,) + (1,) * (len(dims) - 1 - dim))
    return factor_of


def assign_block(key, own, number, rows, amount, top, reach, skew):
    ranking = jax.random.permutation(key, amount)
    packed, usual = portions_of(amount, rows * top, reach, skew, True), portions_of(amount, rows * top, reach, skew, False)
    places = jnp.arange(amount)

    def named(sizes, offset_by):
        used = int((sizes > 0).sum())
        fixed = max(1, used // 4)
        passed = fixed + (places - fixed + offset_by * (used - fixed)) % max(1, amount - fixed)
        return jnp.zeros((amount,), jnp.int32).at[ranking[jnp.where(places < fixed, places, passed)]].set(jnp.asarray(sizes, jnp.int32))

    sizes = jnp.where(number % 4 == 0, named(packed, number // 4), named(usual, number - number // 4 - 1))
    mixed = jax.random.permutation(jax.random.fold_in(own, 3), amount)
    giver, taker = mixed[0:amount // 2 * 2:2], mixed[1:amount // 2 * 2:2]
    room = jnp.minimum(sizes[giver] - 1, reach - sizes[taker]) // 2
    room = jnp.where((giver == ranking[0]) | (taker == ranking[0]) | (sizes[taker] == 0), 0, jnp.maximum(room, 0))
    passed = jax.random.randint(jax.random.fold_in(own, 4), (amount // 2,), 0, 1 << 20) % (room + 1)
    sizes = sizes.at[giver].add(-passed).at[taker].add(passed)
    labels = jnp.searchsorted(jnp.cumsum(sizes), jnp.arange(rows * top), side="right").astype(jnp.int32)
    grid = labels.reshape(top, rows).T
    grid = grid[jax.random.permutation(jax.random.fold_in(own, 1), rows)]
    offset_by = jax.random.randint(jax.random.fold_in(own, 2), (rows, 1), 0, top)
    return jnp.take_along_axis(grid, (jnp.arange(top)[None, :] + offset_by) % top, axis=1)


def portions_of(number_of, total, most, lean, full):
    weights = [(1 << 20) // math.isqrt(standing ** lean) + 1 for standing in range(1, number_of + 1)]
    largest = most if full else min(most, max(-(-total // number_of), total * weights[0] // sum(weights)))
    least = 1 if total - largest >= number_of - 1 else 0
    holding, surplus = [largest] + [least] * (number_of - 1), total - largest - least * (number_of - 1)
    while surplus > 0:
        candidates = [i for i in range(1, number_of) if holding[i] < largest] or [i for i in range(1, number_of) if holding[i] < most]
        mass, left = sum([weights[i] for i in candidates]), surplus
        for i in candidates:
            addition = min(most - holding[i], max(1, left * weights[i] // mass), surplus)
            holding[i] = holding[i] + addition
            surplus = surplus - addition
    return np.array(holding)


def gaussian(key, shape, spread, bound, shards=(), dtype=jnp.bfloat16):
    loudness = block_scale(key, shape, shards, -0.22, 0.18) if shards else 1.0
    drawn = jax.random.normal(key, shape, jnp.float32) * spread * loudness
    return jnp.minimum(jnp.maximum(drawn, -bound), bound).astype(dtype)


def setup_inputs(seed: int = 0) -> dict:
    splits = jax.random.split(jax.random.key(seed), 5)
    documents = gaussian(splits[0], (DOCS, E), 2.0, 12.0, ((0, 32),))
    owner_tile_keys = jax.random.split(jax.random.fold_in(splits[1], 1), DOCS // DOC_DEV)
    owner_tile_turns = jax.random.permutation(jax.random.fold_in(splits[1], 3), DOCS // DOC_DEV)
    owner_tile = jax.vmap(lambda own, number: assign_block(jax.random.fold_in(splits[1], 2), own, number, DOC_DEV, TILES, 1, CAP, 2))(owner_tile_keys, owner_tile_turns).reshape((DOCS, 1))
    unit_in_tile = with_ends(jax.random.randint(splits[2], (DOCS,), 0, TR * TC), jax.random.fold_in(splits[2], 1), 0, (TR * TC) - 1).astype(jnp.int32)
    codebook = gaussian(splits[3], (MR, MC, E), 1.0, 6.0, ((0, 8), (1, 4)))
    return {"documents": documents, "owner_tile": owner_tile, "unit_in_tile": unit_in_tile, "codebook": codebook}


def smooth_along(values_in, axis_dim, extent):
    weights = [math.exp(-2.0 * shift_k * shift_k / RADIUS ** 2) for shift_k in range(-RADIUS, RADIUS + 1)]
    pads = [(0, 0)] * values_in.ndim
    pads[axis_dim] = (RADIUS, RADIUS)
    padded = jnp.pad(values_in, pads)
    result = weights[0] * lax.slice_in_dim(padded, 0, extent, axis=axis_dim)
    for place in range(1, 2 * RADIUS + 1):
        result = result + weights[place] * lax.slice_in_dim(padded, place, place + extent, axis=axis_dim)
    return result


def smooth_map(values_in):
    return smooth_along(smooth_along(values_in, 0, MR), 1, MC)


def reference(documents, owner_tile, unit_in_tile, codebook):
    tile_of = owner_tile[:, 0]
    win_row = (tile_of // N_MY) * TR + unit_in_tile // TC
    win_col = (tile_of % N_MY) * TC + unit_in_tile % TC
    flat_unit = (win_row * MC + win_col).astype(jnp.int32)
    hits = jax.ops.segment_sum(jnp.ones((DOCS,), jnp.float32), flat_unit, MR * MC).reshape(MR, MC)
    smooth_hits = smooth_map(hits)
    block_width = 128 if E % 128 == 0 else E
    block_count = E // block_width
    docs_blocks = documents.reshape(DOCS, block_count, block_width).transpose(1, 0, 2)
    code_blocks = codebook.reshape(MR, MC, block_count, block_width).transpose(2, 0, 1, 3)

    def one_block(pieces):
        doc_part, code_part = pieces
        numerator = jax.ops.segment_sum(doc_part.astype(jnp.float32), flat_unit, MR * MC).reshape(MR, MC, block_width)
        smoothed = smooth_map(numerator)
        updated = (smoothed + 8.0 * code_part.astype(jnp.float32)) / (smooth_hits[:, :, None] + 8.0)
        return updated.astype(jnp.bfloat16)

    blocks_out = lax.map(one_block, (docs_blocks, code_blocks))
    return blocks_out.transpose(1, 2, 0, 3).reshape(MR, MC, E)
```

```python
import functools
import math

import jax
import jax.numpy as jnp
import numpy as np
from jax import lax
from jax.experimental import pallas as pl
from jax.experimental.pallas import tpu as pltpu
from jax.sharding import PartitionSpec as P

RADIUS = 8
CHUNKS = 3
WEIGHTS = [math.exp(-2.0 * k * k / RADIUS**2) for k in range(-RADIUS, RADIUS + 1)]
AXES = ("mx", "my")


def pack_kernel(tiles, cap, cols, block, own_ref, unit_ref, docs_ref, marks_ref, *rest):
    outs, place_ref = rest[:-1], rest[-1]
    count = docs_ref.shape[0]
    step = pl.program_id(0)

    @pl.when(step == 0)
    def _():
        own = own_ref[...]
        tile = lax.broadcasted_iota(jnp.int32, (tiles, count), 0)
        mine = jnp.where(tile == own, 1.0, 0.0)
        before = lax.broadcasted_iota(jnp.int32, (count, count), 0)
        after = lax.broadcasted_iota(jnp.int32, (count, count), 1)
        tri = jnp.where(before < after, 1.0, 0.0).astype(jnp.bfloat16)
        earlier = jnp.dot(mine.astype(jnp.bfloat16), tri, preferred_element_type=jnp.float32)
        slot = jnp.sum(mine * earlier, axis=0, keepdims=True)
        place_ref[...] = own * cap + slot.astype(jnp.int32)

    here = lax.broadcasted_iota(jnp.int32, (block, count), 0) + step * block
    pick = jnp.where(here == place_ref[...], 1.0, 0.0).astype(jnp.bfloat16)
    unit = unit_ref[...]
    line = lax.broadcasted_iota(jnp.int32, (16, count), 0)
    mark = jnp.where(line == 0, unit // cols + 1, jnp.where(line == 1, unit % cols + 1, 0))
    marks_ref[...] = lax.dot_general(
        mark.astype(jnp.float32).astype(jnp.bfloat16),
        pick,
        (((1,), (1,)), ((), ())),
        preferred_element_type=jnp.float32,
    ).astype(jnp.bfloat16)
    width = outs[0].shape[1]
    for k, out in enumerate(outs):
        out[...] = jnp.dot(
            pick, docs_ref[:, k * width : (k + 1) * width], preferred_element_type=jnp.float32
        ).astype(jnp.bfloat16)


def pack(own, unit, docs, tiles, cap, cols):
    count, feature = docs.shape
    slots, width = tiles * cap, feature // CHUNKS
    block = 256
    return pl.pallas_call(
        functools.partial(pack_kernel, tiles, cap, cols, block),
        grid=(slots // block,),
        in_specs=[
            pl.BlockSpec((1, count), lambda i: (0, 0)),
            pl.BlockSpec((1, count), lambda i: (0, 0)),
            pl.BlockSpec((count, feature), lambda i: (0, 0)),
        ],
        out_specs=[pl.BlockSpec((16, block), lambda i: (0, i))]
        + [pl.BlockSpec((block, width), lambda i: (i, 0))] * CHUNKS,
        out_shape=[jax.ShapeDtypeStruct((16, slots), jnp.bfloat16)]
        + [jax.ShapeDtypeStruct((slots, width), jnp.bfloat16)] * CHUNKS,
        scratch_shapes=[pltpu.VMEM((1, count), jnp.int32)],
        compiler_params=pltpu.CompilerParams(vmem_limit_bytes=40 << 20),
        cost_estimate=pl.CostEstimate(
            flops=2 * slots * count * feature, bytes_accessed=6 << 20, transcendentals=0
        ),
        name="pack",
    )(own, unit, docs)


def gather_kernel(block, ids_ref, docs_ref, num_ref):
    here = lax.broadcasted_iota(jnp.int32, (block, ids_ref.shape[1]), 0)
    hot = jnp.where(here == ids_ref[...] - pl.program_id(0) * block, 1.0, 0.0)
    num_ref[...] = jnp.dot(
        hot.astype(jnp.bfloat16), docs_ref[...], preferred_element_type=jnp.float32
    )


def accumulate(ids, docs, units):
    slots, width = docs.shape
    block = min(512, units)
    return pl.pallas_call(
        functools.partial(gather_kernel, block),
        grid=(units // block,),
        in_specs=[
            pl.BlockSpec((1, slots), lambda i: (0, 0)),
            pl.BlockSpec((slots, width), lambda i: (0, 0)),
        ],
        out_specs=pl.BlockSpec((block, width), lambda i: (i, 0)),
        out_shape=jax.ShapeDtypeStruct((units, width), jnp.float32),
        compiler_params=pltpu.CompilerParams(vmem_limit_bytes=40 << 20),
        cost_estimate=pl.CostEstimate(
            flops=2 * units * slots * width, bytes_accessed=5 << 20, transcendentals=0
        ),
        name="accumulate",
    )(ids, docs)


def smooth_kernel(
    num_ref, top_ref, bot_ref, left_ref, right_ref, band_ref, inv_ref, code_ref, *rest
):
    out_ref, ext, split = rest[-3:]
    rows, cols, width = num_ref.shape
    tall, wide = rows + 2 * RADIUS, cols + 2 * RADIUS
    ext[0:RADIUS, RADIUS : RADIUS + cols, :] = top_ref[...].astype(jnp.float32)
    ext[RADIUS : RADIUS + rows, RADIUS : RADIUS + cols, :] = num_ref[...]
    ext[RADIUS + rows :, RADIUS : RADIUS + cols, :] = bot_ref[...].astype(jnp.float32)
    ext[:, 0:RADIUS, :] = left_ref[...].astype(jnp.float32)
    ext[:, RADIUS + cols :, :] = right_ref[...].astype(jnp.float32)
    group, lanes, high = 4, 128, 16

    def down(step, carry):
        base = step * group
        for c in range(0, wide, high):
            for f in range(0, width, lanes):
                x = [
                    ext[base + i, c : c + high, f : f + lanes] for i in range(group + 2 * RADIUS)
                ]
                for g in range(group):
                    total = x[g + RADIUS]
                    for k in range(RADIUS):
                        total = total + WEIGHTS[k] * (x[g + k] + x[g + 2 * RADIUS - k])
                    main = total.astype(jnp.bfloat16)
                    small = (total - main.astype(jnp.float32)).astype(jnp.bfloat16)
                    split[base + g, c : c + high, f : f + lanes] = main
                    split[base + g, wide + c : wide + c + high, f : f + lanes] = small
                    split[base + g, 2 * wide + c : 2 * wide + c + high, f : f + lanes] = main
        return carry

    lax.fori_loop(0, rows // group, down, 0)

    def across(step, carry):
        for g in range(2):
            r = step * 2 + g
            y = jnp.dot(band_ref[...], split[r], preferred_element_type=jnp.float32)
            inv = inv_ref[r]
            for f in range(0, width, lanes):
                code = code_ref[r, :, f : f + lanes].astype(jnp.float32)
                out_ref[r, :, f : f + lanes] = (
                    (y[:, f : f + lanes] + 8.0 * code) * inv
                ).astype(jnp.bfloat16)
        return carry

    lax.fori_loop(0, rows // 2, across, 0)


def smooth(part, num, top, bot, left, right, band, inv, codebook, result):
    rows, cols, width = num.shape
    feature = codebook.shape[2]
    block = 256 if width % 256 == 0 else width
    first = part * (width // block)
    tall, wide = rows + 2 * RADIUS, cols + 2 * RADIUS

    def spec(a, b, offset=0):
        return pl.BlockSpec((a, b, block), lambda i: (0, 0, i + offset))

    held = [] if result is None else [result]
    return pl.pallas_call(
        smooth_kernel,
        grid=(width // block,),
        in_specs=[
            spec(rows, cols),
            spec(RADIUS, cols),
            spec(RADIUS, cols),
            spec(tall, RADIUS),
            spec(tall, RADIUS),
            pl.BlockSpec(band.shape, lambda i: (0, 0)),
            pl.BlockSpec(inv.shape, lambda i: (0, 0, 0)),
            spec(rows, cols, first),
        ]
        + [pl.BlockSpec(memory_space=pl.ANY)] * len(held),
        out_specs=spec(rows, cols, first),
        out_shape=jax.ShapeDtypeStruct((rows, cols, feature), jnp.bfloat16),
        input_output_aliases={8: 0} if held else {},
        scratch_shapes=[
            pltpu.VMEM((tall, wide, block), jnp.float32),
            pltpu.VMEM((rows, 3 * wide, block), jnp.bfloat16),
        ],
        compiler_params=pltpu.CompilerParams(vmem_limit_bytes=56 << 20),
        cost_estimate=pl.CostEstimate(
            flops=12 * 10**9 // CHUNKS, bytes_accessed=30 * 2**20 // CHUNKS, transcendentals=0
        ),
        name="smooth",
    )(num, top, bot, left, right, band, inv, codebook, *held)


def shifts(axis):
    n = lax.axis_size(axis)
    up = [(i, i + 1) for i in range(n - 1)]
    return up, [(j, i) for i, j in up]


def halo(x, dtype):
    rows, cols = x.shape[:2]
    up, down = shifts("mx")
    top = lax.ppermute(x[rows - RADIUS :].astype(dtype), "mx", up)
    bot = lax.ppermute(x[:RADIUS].astype(dtype), "mx", down)
    up, down = shifts("my")

    def side(a, b):
        return jnp.concatenate([top[:, a:b], x[:, a:b].astype(dtype), bot[:, a:b]], axis=0)

    left = lax.ppermute(side(cols - RADIUS, cols), "my", up)
    right = lax.ppermute(side(0, RADIUS), "my", down)
    return top, bot, left, right


def banded(extent):
    full = np.zeros((extent, extent + 2 * RADIUS), np.float32)
    for r in range(extent):
        full[r, r : r + 2 * RADIUS + 1] = WEIGHTS
    return full


def on_device(documents, owner_tile, unit_in_tile, codebook):
    tiles = lax.axis_size("mx") * lax.axis_size("my")
    rows, cols, feature = codebook.shape
    count = documents.shape[0]
    cap = max(2, 2 * count // tiles)
    marks, *sent = pack(
        owner_tile.reshape(1, count), unit_in_tile.reshape(1, count), documents, tiles, cap, cols
    )

    def exchange(x, axis):
        return lax.all_to_all(x, AXES, split_axis=axis, concat_axis=axis, tiled=True)

    marks = exchange(marks[:2].reshape(2, tiles, cap), 1).reshape(2, tiles * cap)
    got = [exchange(x.reshape(tiles, cap, -1), 0).reshape(tiles * cap, -1) for x in sent]
    spot = marks.astype(jnp.int32) - 1
    ids = jnp.where(spot[0] < 0, -1, spot[0] * cols + spot[1])[None, :]
    in_row = (spot[0][None, :] == jnp.arange(rows)[:, None]).astype(jnp.bfloat16)
    in_col = (spot[1][None, :] == jnp.arange(cols)[:, None]).astype(jnp.bfloat16)
    hits = lax.dot_general(
        in_row, in_col, (((1,), (1,)), ((), ())), preferred_element_type=jnp.float32
    )
    top, bot, left, right = halo(hits, jnp.float32)
    hits = jnp.concatenate([left, jnp.concatenate([top, hits, bot], 0), right], 1)
    exact = lax.Precision.HIGHEST
    hits = jnp.dot(
        jnp.dot(jnp.asarray(banded(rows)), hits, precision=exact),
        jnp.asarray(banded(cols).T),
        precision=exact,
    )
    inv = jnp.broadcast_to((1.0 / (hits + 8.0))[:, :, None], (rows, cols, 128))
    full = banded(cols)
    main = full.astype(jnp.bfloat16)
    small = (full - main.astype(np.float32)).astype(jnp.bfloat16)
    band = jnp.asarray(np.concatenate([main, main, small], axis=1))

    result = None
    for part, docs in enumerate(got):
        num = accumulate(ids, docs, rows * cols).reshape(rows, cols, -1)
        result = smooth(part, num, *halo(num, jnp.bfloat16), band, inv, codebook, result)
    return result


def solution(mesh):
    return jax.shard_map(
        on_device,
        mesh=mesh,
        in_specs=(P(AXES, None), P(AXES, None), P(AXES), P("mx", "my", None)),
        out_specs=P("mx", "my", None),
        check_vma=False,
    )
```
